32 devices in a mesh: ctx: 8 (over z, x), tp: 4 (over y, core).
Axes of the slice: x: 2, y: 2, z: 4, core: 2. Of those that a mesh axis runs over, the one named last changes fastest.
Arguments:
- queries: bfloat16 [2048, 4096], P('ctx', 'tp'), may hold values from -8 to 8
- keys_values: bfloat16 [2048, 2, 512], P('ctx', None, 'tp'), may hold values from -8 to 8
- placement: int32 [2], replicated, may hold values from 1 to 7
- lengths: int32 [8], replicated, may hold values from 1 to 1365, 2048 in all
- steer_index: int32 [8], replicated, may hold values from 0 to 15
- steering: bfloat16 [16, 4096], P(None, 'tp'), may hold values from -3 to 3
Outputs:
- steered: bfloat16 [2048, 4096], P('ctx', 'tp')
The draws below stay inside these ranges and needn't reach their ends.
Inputs may be any that keep to these rules, and one draw needn't show every extreme that they name: The lengths sum to 2048 and the longest is exactly 1365.
All inputs are finite; a program needn't handle non-finite values.
Results may differ from the reference program's by a relative error of at most 0.0034.
Values may be sent and summed in bfloat16 or wider, within the bound.
A program may use at most 64 MiB of HBM per device.

```python
import math
import jax
import jax.numpy as jnp
import numpy as np
from jax import lax

HEADS = 32
KVH = 4
HD = 128
NREQ = 8
NSTEER = 16
TOKENS = 2048
MOST = 1365
BQ = 512
N_CTX = 8


def draw_keys_values(key, part):
    shape_all = (TOKENS, 2, KVH * HD)
    baseline = jnp.clip(jax.random.normal(jax.random.fold_in(key, 11), shape_all, jnp.float32), -6.0, 6.0)
    return baseline.astype(jnp.bfloat16)


def draw_queries(key, part):
    shape_all = (TOKENS, HEADS * HD)
    baseline = jnp.clip(jax.random.normal(jax.random.fold_in(key, 13), shape_all, jnp.float32), -6.0, 6.0)
    return baseline.astype(jnp.bfloat16)


def plant(result, rng, low, high):
    shape = result.shape
    index_at = [jax.random.randint(jax.random.fold_in(rng, axis), (), 0, shape[axis]) for axis in range(len(shape))]
    result = result.at[tuple(index_at)].set(low)
    longest = shape.index(max(shape))
    index_at[longest] = (index_at[longest] + 1) % shape[longest]
    return result.at[tuple(index_at)].set(high)


def block_scale(rng, dims, pieces, low, top_value):
    gain = 1.0
    for dim, blocks in pieces:
        draws = jax.random.uniform(jax.random.fold_in(jax.random.fold_in(rng, 6), dim), (blocks,), jnp.float32, low / len(pieces), top_value / len(pieces))
        gain = gain * jnp.repeat(jnp.exp(draws), dims[dim] // blocks).reshape((-1,) + (1,) * (len(dims) - 1 - dim))
    return gain


def profile(count, total, limit, skew):
    portions = [(1 << 20) // math.isqrt(grade ** skew) + 1 for grade in range(2, count + 1)]
    spare, holding = total - limit - (count - 1), [1] * (count - 1)
    while spare > 0:
        movable = [i for i in range(count - 1) if holding[i] < limit]
        whole, remaining = sum([portions[i] for i in movable]), spare
        for i in movable:
            extra = min(limit - holding[i], max(1, remaining * portions[i] // whole), spare)
            holding[i] = holding[i] + extra
            spare = spare - extra
    return np.array([limit] + holding)


def ragged(own_key, amount, total, most, slope):
    if amount == 2:
        one = jax.random.randint(own_key, (), max(1, total - most), min(most, total - 1) + 1)
        return jnp.stack([one, total - one])
    sizes = jnp.asarray(profile(amount, total, most, slope), jnp.int32)
    pairs = (amount - 1) // 2
    source_of, taker = sizes[1:1 + 2 * pairs:2], sizes[2:2 + 2 * pairs:2]
    room = jnp.minimum(source_of - 1, most - taker)
    passed = jax.random.randint(jax.random.fold_in(own_key, 1), (pairs,), 0, 1 << 20) % (room + 1)
    sizes = sizes.at[1:1 + 2 * pairs:2].set(source_of - passed).at[2:2 + 2 * pairs:2].set(taker + passed)
    return sizes[jax.random.permutation(jax.random.fold_in(own_key, 2), amount)]


def gaussian(own_key, extent, scale, reach, split=(), kind=jnp.bfloat16):
    drawn = scale * jax.random.normal(own_key, extent, jnp.float32)
    if split:
        drawn = drawn * block_scale(own_key, extent, split, -0.22, 0.18)
    return jnp.clip(drawn, -reach, reach).astype(kind)


def setup_inputs(seed: int = 0) -> dict:
    arg_keys = jax.random.split(jax.random.key(seed), 7)
    queries = draw_queries(jax.random.fold_in(arg_keys[6], 71), 0)
    keys_values = draw_keys_values(jax.random.fold_in(arg_keys[6], 71), 0)
    placement = jax.random.randint(arg_keys[2], (2,), 1, N_CTX).astype(jnp.int32)
    lengths = ragged(arg_keys[3], NREQ, TOKENS, MOST, 2).astype(jnp.int32)
    steer_index = plant(jax.random.randint(arg_keys[4], (NREQ,), 0, NSTEER), jax.random.fold_in(arg_keys[4], 1), 0, NSTEER - 1).astype(jnp.int32)
    steering = gaussian(arg_keys[5], (NSTEER, HEADS * HD), 0.5, 3.0, ((1, 4),))
    return {"queries": queries, "keys_values": keys_values, "placement": placement, "lengths": lengths, "steer_index": steer_index, "steering": steering}


def packed_positions(placement, tok_rows, shards):
    shard_ids = jnp.arange(shards, dtype=jnp.int32)
    local_rows = jnp.arange(tok_rows, dtype=jnp.int32)
    half_rows = tok_rows // 2
    mask_rows = jnp.where(local_rows < half_rows, placement[0], placement[1]).astype(jnp.int32)
    owners = jnp.bitwise_xor(shard_ids[:, None], mask_rows[None, :]).astype(jnp.int32)
    return (owners * tok_rows + local_rows[None, :]).reshape(-1).astype(jnp.int32)


def request_of(positions, lengths):
    request_ends = jnp.cumsum(lengths).astype(jnp.int32)
    return jnp.sum((positions[:, None] >= request_ends[None, :]).astype(jnp.int32), axis=1).astype(jnp.int32)


def reference(queries, keys_values, placement, lengths, steer_index, steering):
    tok_rows = TOKENS // N_CTX
    positions = packed_positions(placement, tok_rows, N_CTX)
    q_packed = jnp.zeros_like(queries).at[positions].set(queries)
    kv_packed = jnp.zeros_like(keys_values).at[positions].set(keys_values)
    request = request_of(jnp.arange(TOKENS, dtype=jnp.int32), lengths)
    group_size = HEADS // KVH
    window = MOST + BQ
    scale = HD ** -0.5

    def one_block(block_index):
        row_first = (block_index * BQ).astype(jnp.int32)
        key_first = jnp.clip(row_first - MOST, 0, TOKENS - window).astype(jnp.int32)
        query_block = lax.dynamic_slice_in_dim(q_packed, row_first, BQ, 0).astype(jnp.float32).reshape(BQ, KVH, group_size, HD)
        kv_block = lax.dynamic_slice_in_dim(kv_packed, key_first, window, 0).astype(jnp.float32)
        key_rows = kv_block[:, 0].reshape(window, KVH, HD)
        value_rows = kv_block[:, 1].reshape(window, KVH, HD)
        query_pos = row_first + jnp.arange(BQ, dtype=jnp.int32)
        key_pos = key_first + jnp.arange(window, dtype=jnp.int32)
        query_request = lax.dynamic_slice_in_dim(request, row_first, BQ, 0)
        key_request = lax.dynamic_slice_in_dim(request, key_first, window, 0)
        allowed = (query_request[:, None] == key_request[None, :]) & (key_pos[None, :] <= query_pos[:, None])
        allowed = allowed[:, None, None, :]
        scores = jnp.einsum("qhgd,khd->qhgk", query_block, key_rows) * scale
        masked = jnp.where(allowed, scores, jnp.float32(-1.0e30))
        row_max = jnp.max(masked, axis=-1, keepdims=True)
        weights = jnp.where(allowed, jnp.exp(masked - row_max), jnp.float32(0.0))
        weight_total = jnp.sum(weights, axis=-1)
        rounded = lax.optimization_barrier(weights.astype(jnp.bfloat16)).astype(jnp.float32)
        mixed = jnp.einsum("qhgk,khd->qhgd", rounded, value_rows)
        return (mixed / weight_total[..., None]).reshape(BQ, HEADS * HD).astype(jnp.bfloat16)

    attended = lax.map(one_block, jnp.arange(TOKENS // BQ, dtype=jnp.int32)).reshape(TOKENS, HEADS * HD)
    chosen = jnp.sum(jnp.where(request[:, None] == jnp.arange(NREQ, dtype=jnp.int32)[None, :], steer_index[None, :], 0), axis=1).astype(jnp.int32)
    steer_rows = steering[chosen].astype(jnp.float32)
    return (attended.astype(jnp.float32) + steer_rows).astype(jnp.bfloat16)
```

```python
import functools
import math

import jax
import jax.numpy as jnp
from jax import lax
from jax.experimental import pallas as pl
from jax.experimental.pallas import tpu as pltpu
from jax.sharding import PartitionSpec as P

HD = 128
FILL = -1e30
FACTOR = math.log2(math.e) / math.sqrt(HD)
MESH = pl.DeviceIdType.MESH


def flip(value, mask):
    result = value
    bit = 1
    while bit <= mask:
        if mask & bit:
            result = result + bit * (1 - 2 * lax.rem(lax.div(value, bit), 2))
        bit *= 2
    return result


def move_kernel(shards, masks, q_ref, kv_ref, q_out, kv_out, own_sem, q_send, q_recv, kv_send, kv_recv):
    me = lax.axis_index("ctx")
    barrier = pltpu.get_barrier_semaphore()
    for away in range(1, shards):
        pl.semaphore_signal(
            barrier, inc=1, device_id={"ctx": lax.rem(me + away, shards)}, device_id_type=MESH
        )
    pl.semaphore_wait(barrier, shards - 1)

    half = q_ref.shape[0] // 2
    line = shards // 2
    x, z = lax.rem(me, 2), lax.div(me, 2)
    beside = me + 1 - 2 * x
    targets = (beside, me + 2, me - 2)

    def place(source, j):
        return kv_out.at[:, flip(source, masks[j]) * 2 + j]

    def copy(source, j, way, own=False):
        return pltpu.make_async_remote_copy(
            src_ref=kv_ref.at[:, j] if own else place(source, j),
            dst_ref=place(source, j),
            send_sem=kv_send.at[source, way, j],
            recv_sem=kv_recv.at[source, j],
            device_id={"ctx": targets[way]},
            device_id_type=MESH,
        )

    def query_copy(j):
        rows = pl.ds(j * half, half)
        return pltpu.make_async_remote_copy(
            src_ref=q_ref.at[rows],
            dst_ref=q_out.at[rows],
            send_sem=q_send.at[j],
            recv_sem=q_recv.at[j],
            device_id={"ctx": flip(me, masks[j])},
            device_id_type=MESH,
        )

    can_up, can_down = z < line - 1, z > 0
    for j in range(2):
        pl.when(can_up)(lambda j=j: copy(me, j, 1, True).start())
        pl.when(can_down)(lambda j=j: copy(me, j, 2, True).start())
        copy(me, j, 0, True).start()
    for j in range(2):
        query_copy(j).start()
        pltpu.make_async_copy(kv_ref.at[:, j], place(me, j), own_sem.at[j]).start()

    for step in range(1, line):
        for j in range(2):

            @pl.when(z >= step)
            def _():
                source = me - 2 * step
                copy(source, j, 1).wait_recv()
                pl.when(can_up)(lambda: copy(source, j, 1).start())
                copy(source, j, 0).start()

            @pl.when(z + step < line)
            def _():
                source = me + 2 * step
                copy(source, j, 2).wait_recv()
                pl.when(can_down)(lambda: copy(source, j, 2).start())
                copy(source, j, 0).start()

    for level in range(line):
        for j in range(2):
            copy(level * 2 + 1 - x, j, 0).wait_recv()
    for j in range(2):
        query_copy(j).wait_recv()
        query_copy(j).wait_send()
        pltpu.make_async_copy(kv_ref.at[:, j], place(me, j), own_sem.at[j]).wait()
        pl.when(can_up)(lambda j=j: copy(me, j, 1, True).wait_send())
        pl.when(can_down)(lambda j=j: copy(me, j, 2, True).wait_send())
        copy(me, j, 0, True).wait_send()
        for step in range(1, line):

            @pl.when(z >= step)
            def _():
                source = me - 2 * step
                pl.when(can_up)(lambda: copy(source, j, 1).wait_send())
                copy(source, j, 0).wait_send()

            @pl.when(z + step < line)
            def _():
                source = me + 2 * step
                pl.when(can_down)(lambda: copy(source, j, 2).wait_send())
                copy(source, j, 0).wait_send()


def move(shards, masks, queries, own_kv):
    rows, width = queries.shape
    return pl.pallas_call(
        functools.partial(move_kernel, shards, masks),
        out_shape=(
            jax.ShapeDtypeStruct((rows, width), jnp.bfloat16),
            jax.ShapeDtypeStruct((2, 2 * shards, rows // 2, own_kv.shape[3]), jnp.bfloat16),
        ),
        in_specs=[pl.BlockSpec(memory_space=pl.ANY)] * 2,
        out_specs=(pl.BlockSpec(memory_space=pl.ANY),) * 2,
        scratch_shapes=[
            pltpu.SemaphoreType.DMA((2,)),
            pltpu.SemaphoreType.DMA((2,)),
            pltpu.SemaphoreType.DMA((2,)),
            pltpu.SemaphoreType.DMA((shards, 3, 2)),
            pltpu.SemaphoreType.DMA((shards, 2)),
        ],
        compiler_params=pltpu.CompilerParams(
            collective_id=(masks[0] - 1) * (shards - 1) + masks[1] - 1, has_side_effects=True
        ),
        name=f"move_{masks[0]}_{masks[1]}",
    )(queries, own_kv)


def attend_kernel(lengths, steer_index, q_ref, kv_ref, steering_ref, out_ref, acc, top, total):
    me = lax.axis_index("ctx")
    rows = q_ref.shape[0]
    heads = q_ref.shape[1] // HD
    requests = lengths.shape[0]
    first = me * rows
    ends = []
    for r in range(requests):
        ends.append(lengths[r] + (ends[-1] if r else 0))

    row_pos = first + lax.broadcasted_iota(jnp.int32, (1, rows), 1)
    row_start = jnp.zeros((1, rows), jnp.int32)
    first_start = jnp.int32(0)
    for r in range(requests):
        row_start = row_start + jnp.where(row_pos >= ends[r], lengths[r], 0)
        first_start = first_start + jnp.where(first >= ends[r], lengths[r], 0)

    top[...] = jnp.full(top.shape, FILL, jnp.float32)
    total[...] = jnp.zeros(total.shape, jnp.float32)
    acc[...] = jnp.zeros(acc.shape, jnp.float32)

    def block(index, carry):
        at = pl.multiple_of(index * rows, rows)
        key = kv_ref[0, pl.ds(at, rows), :]
        value_t = kv_ref[1, pl.ds(at, rows), :].T
        key_pos = at + lax.broadcasted_iota(jnp.int32, (rows, rows), 0)
        bias = jnp.where((key_pos >= row_start) & (key_pos <= row_pos), 0.0, FILL)
        for h in range(heads):
            query = q_ref[:, h * HD : (h + 1) * HD]
            scores = bias + lax.dot_general(
                key, query, (((1,), (1,)), ((), ())), preferred_element_type=jnp.float32
            )
            old = top[h : h + 1, :]
            new = jnp.maximum(old, jnp.max(scores, axis=0, keepdims=True))
            weights = jnp.exp2((scores - new) * FACTOR)
            rescale = jnp.exp2((old - new) * FACTOR)
            top[h : h + 1, :] = new
            total[h : h + 1, :] = total[h : h + 1, :] * rescale + jnp.sum(
                weights, axis=0, keepdims=True
            )
            acc[h] = acc[h] * rescale + jnp.dot(
                value_t, weights.astype(jnp.bfloat16), preferred_element_type=jnp.float32
            )
        return carry

    lax.fori_loop(lax.div(first_start, rows), me + 1, block, 0)

    vectors = steering_ref.shape[0]
    pos = first + lax.broadcasted_iota(jnp.int32, (rows, vectors), 0)
    chosen = jnp.zeros((rows, vectors), jnp.int32)
    for r in range(requests):
        inside = (pos >= ends[r] - lengths[r]) & (pos < ends[r])
        chosen = jnp.where(inside, steer_index[r], chosen)
    one_hot = (chosen == lax.broadcasted_iota(jnp.int32, (rows, vectors), 1)).astype(jnp.bfloat16)
    for h in range(heads):
        columns = slice(h * HD, (h + 1) * HD)
        mixed = (acc[h] * (1.0 / total[h : h + 1, :])).T.astype(jnp.bfloat16)
        steer = jnp.dot(one_hot, steering_ref[:, columns], preferred_element_type=jnp.float32)
        out_ref[:, columns] = (mixed.astype(jnp.float32) + steer).astype(jnp.bfloat16)


def attend(queries, kv, lengths, steer_index, steering):
    rows, width = queries.shape
    heads = width // HD
    vmem = pl.BlockSpec(memory_space=pltpu.VMEM)
    smem = pl.BlockSpec(memory_space=pltpu.SMEM)
    return pl.pallas_call(
        attend_kernel,
        out_shape=jax.ShapeDtypeStruct((rows, width), jnp.bfloat16),
        in_specs=[smem, smem, vmem, vmem, vmem],
        out_specs=vmem,
        scratch_shapes=[
            pltpu.VMEM((heads, HD, rows), jnp.float32),
            pltpu.VMEM((heads, rows), jnp.float32),
            pltpu.VMEM((heads, rows), jnp.float32),
        ],
        compiler_params=pltpu.CompilerParams(vmem_limit_bytes=48 * 2**20),
        name="attend",
    )(lengths, steer_index, queries, kv, steering)


def move_by_bits(shards, queries, own_kv, placement):
    rows = queries.shape[0]
    first_half = jnp.arange(rows) < rows // 2
    bit = 1
    while bit < shards:
        pairs = [(source, source ^ bit) for source in range(shards)]
        moved = lax.ppermute(queries, "ctx", pairs)
        flags = (placement // bit) % 2
        queries = jnp.where(
            (jnp.where(first_half, flags[0], flags[1]) == 1)[:, None], moved, queries
        )
        bit *= 2
    kv = lax.all_gather(own_kv, "ctx", axis=1)
    ids = jnp.arange(shards, dtype=jnp.int32)
    halves = [jnp.take(kv[:, :, j], ids ^ placement[j], axis=1) for j in range(2)]
    return queries, jnp.stack(halves, axis=2)


def body(queries, keys_values, placement, lengths, steer_index, steering):
    shards = lax.axis_size("ctx")
    rows = queries.shape[0]
    depth = keys_values.shape[2]
    own_kv = keys_values.transpose(1, 0, 2).reshape(2, 2, rows // 2, depth)
    if shards <= 8:
        count = shards - 1
        branches = [
            functools.partial(move, shards, (1 + i // count, 1 + i % count))
            for i in range(count * count)
        ]
        queries, kv = lax.switch(
            (placement[0] - 1) * count + placement[1] - 1, branches, queries, own_kv
        )
    else:
        queries, kv = move_by_bits(shards, queries, own_kv, placement)
    kv = kv.reshape(2, shards * rows, depth)
    return attend(queries, kv, lengths, steer_index, steering)


def solution(mesh):
    return jax.shard_map(
        body,
        mesh=mesh,
        in_specs=(P("ctx", "tp"), P("ctx", None, "tp"), P(), P(), P(), P(None, "tp")),
        out_specs=P("ctx", "tp"),
        check_vma=False,
    )
```

```python
import functools
import math

import jax
import jax.numpy as jnp
from jax import lax
from jax.experimental import pallas as pl
from jax.experimental.pallas import tpu as pltpu
from jax.sharding import PartitionSpec as P

HD = 128
FILL = -1e30
FACTOR = math.log2(math.e) / math.sqrt(HD)
MESH = pl.DeviceIdType.MESH


def flip(value, mask):
    result = value
    bit = 1
    while bit <= mask:
        if mask & bit:
            result = result + bit * (1 - 2 * lax.rem(lax.div(value, bit), 2))
        bit *= 2
    return result


def move_kernel(shards, masks, q_ref, kv_ref, q_out, kv_out, own_sem, q_send, q_recv, kv_send, kv_recv):
    me = lax.axis_index("ctx")
    barrier = pltpu.get_barrier_semaphore()
    for away in range(1, shards):
        pl.semaphore_signal(
            barrier, inc=1, device_id={"ctx": lax.rem(me + away, shards)}, device_id_type=MESH
        )
    pl.semaphore_wait(barrier, shards - 1)

    half = q_ref.shape[0] // 2
    part = half // q_send.shape[1]
    line = shards // 2
    x, z = lax.rem(me, 2), lax.div(me, 2)
    beside = me + 1 - 2 * x
    targets = (beside, me + 2, me - 2)

    def place(source, j):
        return kv_out.at[:, flip(source, masks[j]) * 2 + j]

    def copy(source, j, way, own=False):
        return pltpu.make_async_remote_copy(
            src_ref=kv_ref.at[:, j] if own else place(source, j),
            dst_ref=place(source, j),
            send_sem=kv_send.at[source, way, j],
            recv_sem=kv_recv.at[source, j],
            device_id={"ctx": targets[way]},
            device_id_type=MESH,
        )

    def query_copy(j, c):
        rows = pl.ds(j * half + c * part, part)
        return pltpu.make_async_remote_copy(
            src_ref=q_ref.at[rows],
            dst_ref=q_out.at[rows],
            send_sem=q_send.at[j, c],
            recv_sem=q_recv.at[j, c],
            device_id={"ctx": flip(me, masks[j])},
            device_id_type=MESH,
        )

    can_up, can_down = z < line - 1, z > 0
    for j in range(2):
        pl.when(can_up)(lambda j=j: copy(me, j, 1, True).start())
        pl.when(can_down)(lambda j=j: copy(me, j, 2, True).start())
        copy(me, j, 0, True).start()
    for j in range(2):
        query_copy(j, 0).start()
        pltpu.make_async_copy(kv_ref.at[:, j], place(me, j), own_sem.at[j]).start()

    for step in range(1, line):
        for j in range(2):

            @pl.when(z >= step)
            def _():
                source = me - 2 * step
                copy(source, j, 1).wait_recv()
                pl.when(can_up)(lambda: copy(source, j, 1).start())
                copy(source, j, 0).start()

            @pl.when(z + step < line)
            def _():
                source = me + 2 * step
                copy(source, j, 2).wait_recv()
                pl.when(can_down)(lambda: copy(source, j, 2).start())
                copy(source, j, 0).start()

        for j in range(2):
            query_copy(j, step).start()

    for level in range(line):
        for j in range(2):
            copy(level * 2 + 1 - x, j, 0).wait_recv()
    for j in range(2):
        for c in range(line):
            query_copy(j, c).wait_recv()
            query_copy(j, c).wait_send()
        pltpu.make_async_copy(kv_ref.at[:, j], place(me, j), own_sem.at[j]).wait()
        pl.when(can_up)(lambda j=j: copy(me, j, 1, True).wait_send())
        pl.when(can_down)(lambda j=j: copy(me, j, 2, True).wait_send())
        copy(me, j, 0, True).wait_send()
        for step in range(1, line):

            @pl.when(z >= step)
            def _():
                source = me - 2 * step
                pl.when(can_up)(lambda: copy(source, j, 1).wait_send())
                copy(source, j, 0).wait_send()

            @pl.when(z + step < line)
            def _():
                source = me + 2 * step
                pl.when(can_down)(lambda: copy(source, j, 2).wait_send())
                copy(source, j, 0).wait_send()


def move(shards, masks, queries, own_kv):
    rows, width = queries.shape
    return pl.pallas_call(
        functools.partial(move_kernel, shards, masks),
        out_shape=(
            jax.ShapeDtypeStruct((rows, width), jnp.bfloat16),
            jax.ShapeDtypeStruct((2, 2 * shards, rows // 2, own_kv.shape[3]), jnp.bfloat16),
        ),
        in_specs=[pl.BlockSpec(memory_space=pl.ANY)] * 2,
        out_specs=(pl.BlockSpec(memory_space=pl.ANY),) * 2,
        scratch_shapes=[
            pltpu.SemaphoreType.DMA((2,)),
            pltpu.SemaphoreType.DMA((2, shards // 2)),
            pltpu.SemaphoreType.DMA((2, shards // 2)),
            pltpu.SemaphoreType.DMA((shards, 3, 2)),
            pltpu.SemaphoreType.DMA((shards, 2)),
        ],
        compiler_params=pltpu.CompilerParams(
            collective_id=(masks[0] - 1) * (shards - 1) + masks[1] - 1, has_side_effects=True
        ),
        name=f"move_{masks[0]}_{masks[1]}",
    )(queries, own_kv)


def attend_kernel(lengths, steer_index, q_ref, kv_ref, steering_ref, out_ref, acc, top):
    me = lax.axis_index("ctx")
    rows = q_ref.shape[0]
    heads = q_ref.shape[1] // HD
    requests = lengths.shape[0]
    first = me * rows
    ends = []
    for r in range(requests):
        ends.append(lengths[r] + (ends[-1] if r else 0))

    row_pos = first + lax.broadcasted_iota(jnp.int32, (rows, 1), 0)
    row_start = jnp.zeros((rows, 1), jnp.int32)
    first_start = jnp.int32(0)
    for r in range(requests):
        row_start = row_start + jnp.where(row_pos >= ends[r], lengths[r], 0)
        first_start = first_start + jnp.where(first >= ends[r], lengths[r], 0)

    top[...] = jnp.full(top.shape, FILL, jnp.float32)
    acc[...] = jnp.zeros(acc.shape, jnp.float32)

    def block(index, carry):
        at = pl.multiple_of(index * rows, rows)
        key = kv_ref[0, pl.ds(at, rows), :]
        value = kv_ref[1, pl.ds(at, rows), :]
        value = jnp.concatenate([value, jnp.ones_like(value)], axis=1)
        key_pos = at + lax.broadcasted_iota(jnp.int32, (rows, rows), 1)
        bias = jnp.where((key_pos >= row_start) & (key_pos <= row_pos), 0.0, FILL)
        for h in range(heads):
            query = q_ref[:, h * HD : (h + 1) * HD]
            scores = bias + lax.dot_general(
                query, key, (((1,), (1,)), ((), ())), preferred_element_type=jnp.float32
            )
            old = top[h]
            new = jnp.maximum(old, jnp.max(scores, axis=1, keepdims=True))
            rescale = jnp.exp2((old - new) * FACTOR)
            top[h] = new
            weights = jnp.exp2((scores - jnp.concatenate([new] * (rows // HD), axis=1)) * FACTOR)
            acc[h] = acc[h] * jnp.concatenate([rescale, rescale], axis=1) + jnp.dot(
                weights.astype(jnp.bfloat16), value, preferred_element_type=jnp.float32
            )
        return carry

    lax.fori_loop(lax.div(first_start, rows), me + 1, block, 0)

    vectors = steering_ref.shape[0]
    pos = first + lax.broadcasted_iota(jnp.int32, (rows, vectors), 0)
    chosen = jnp.zeros((rows, vectors), jnp.int32)
    for r in range(requests):
        inside = (pos >= ends[r] - lengths[r]) & (pos < ends[r])
        chosen = jnp.where(inside, steer_index[r], chosen)
    one_hot = (chosen == lax.broadcasted_iota(jnp.int32, (rows, vectors), 1)).astype(jnp.bfloat16)
    for h in range(heads):
        columns = slice(h * HD, (h + 1) * HD)
        mixed = (acc[h, :, :HD] / acc[h, :, HD:]).astype(jnp.bfloat16)
        steer = jnp.dot(one_hot, steering_ref[:, columns], preferred_element_type=jnp.float32)
        out_ref[:, columns] = (mixed.astype(jnp.float32) + steer).astype(jnp.bfloat16)


def attend(queries, kv, lengths, steer_index, steering):
    rows, width = queries.shape
    heads = width // HD
    vmem = pl.BlockSpec(memory_space=pltpu.VMEM)
    smem = pl.BlockSpec(memory_space=pltpu.SMEM)
    return pl.pallas_call(
        attend_kernel,
        out_shape=jax.ShapeDtypeStruct((rows, width), jnp.bfloat16),
        in_specs=[smem, smem, vmem, vmem, vmem],
        out_specs=vmem,
        scratch_shapes=[
            pltpu.VMEM((heads, rows, 2 * HD), jnp.float32),
            pltpu.VMEM((heads, rows, HD), jnp.float32),
        ],
        compiler_params=pltpu.CompilerParams(vmem_limit_bytes=48 * 2**20),
        name="attend",
    )(lengths, steer_index, queries, kv, steering)


def move_by_bits(shards, queries, own_kv, placement):
    rows = queries.shape[0]
    first_half = jnp.arange(rows) < rows // 2
    bit = 1
    while bit < shards:
        pairs = [(source, source ^ bit) for source in range(shards)]
        moved = lax.ppermute(queries, "ctx", pairs)
        flags = (placement // bit) % 2
        queries = jnp.where(
            (jnp.where(first_half, flags[0], flags[1]) == 1)[:, None], moved, queries
        )
        bit *= 2
    kv = lax.all_gather(own_kv, "ctx", axis=1)
    ids = jnp.arange(shards, dtype=jnp.int32)
    halves = [jnp.take(kv[:, :, j], ids ^ placement[j], axis=1) for j in range(2)]
    return queries, jnp.stack(halves, axis=2)


def choose(branches, low, chosen, *operands):
    if len(branches) == 1:
        return branches[0](*operands)
    middle = len(branches) // 2
    return lax.cond(
        chosen < low + middle,
        functools.partial(choose, branches[:middle], low),
        functools.partial(choose, branches[middle:], low + middle),
        chosen,
        *operands,
    )


def body(queries, keys_values, placement, lengths, steer_index, steering):
    shards = lax.axis_size("ctx")
    rows = queries.shape[0]
    depth = keys_values.shape[2]
    own_kv = keys_values.transpose(1, 0, 2).reshape(2, 2, rows // 2, depth)
    if shards <= 8:
        count = shards - 1
        branches = [
            functools.partial(move, shards, (1 + i // count, 1 + i % count))
            for i in range(count * count)
        ]
        chosen = (placement[0] - 1) * count + placement[1] - 1
        queries, kv = choose(branches, 0, chosen, queries, own_kv)
    else:
        queries, kv = move_by_bits(shards, queries, own_kv, placement)
    kv = kv.reshape(2, shards * rows, depth)
    return attend(queries, kv, lengths, steer_index, steering)


def solution(mesh):
    return jax.shard_map(
        body,
        mesh=mesh,
        in_specs=(P("ctx", "tp"), P("ctx", None, "tp"), P(), P(), P(), P(None, "tp")),
        out_specs=P("ctx", "tp"),
        check_vma=False,
    )
```

```python
import functools
import math

import jax
import jax.numpy as jnp
from jax import lax
from jax.experimental import pallas as pl
from jax.experimental.pallas import tpu as pltpu
from jax.sharding import PartitionSpec as P

HD = 128
FILL = -1e30
FACTOR = math.log2(math.e) / math.sqrt(HD)
MESH = pl.DeviceIdType.MESH


def flip(value, mask):
    result = value
    bit = 1
    while bit <= mask:
        if mask & bit:
            result = result + bit * (1 - 2 * lax.rem(lax.div(value, bit), 2))
        bit *= 2
    return result


def move_kernel(shards, masks, q_ref, kv_ref, q_out, kv_out, own_sem, q_send, q_recv, kv_send, kv_recv):
    me = lax.axis_index("ctx")
    own_copy = pltpu.make_async_copy(kv_ref, kv_out.at[me], own_sem)
    own_copy.start()
    barrier = pltpu.get_barrier_semaphore()

    @pl.loop(1, shards)
    def _(away):
        pl.semaphore_signal(
            barrier, inc=1, device_id={"ctx": lax.rem(me + away, shards)}, device_id_type=MESH
        )

    pl.semaphore_wait(barrier, shards - 1)
    own_copy.wait()

    half = q_ref.shape[0] // 2
    line = shards // 2
    part = half // line
    x, z = lax.rem(me, 2), lax.div(me, 2)
    beside = me + 1 - 2 * x

    def copy(source, way, target):
        return pltpu.make_async_remote_copy(
            src_ref=kv_out.at[source],
            dst_ref=kv_out.at[source],
            send_sem=kv_send.at[source, way],
            recv_sem=kv_recv.at[source],
            device_id={"ctx": target},
            device_id_type=MESH,
        )

    def query_copy(j, c):
        rows = pl.ds(pl.multiple_of(j * half + c * part, part), part)
        return pltpu.make_async_remote_copy(
            src_ref=q_ref.at[rows],
            dst_ref=q_out.at[rows],
            send_sem=q_send.at[j, c],
            recv_sem=q_recv.at[j, c],
            device_id={"ctx": flip(me, masks[j])},
            device_id_type=MESH,
        )

    def within(level):
        return lax.div(level + line, line) == 1

    @pl.loop(0, 2 * line)
    def _(i):
        step, way = lax.div(i, 2), lax.rem(i, 2)
        sign = 1 - 2 * way
        source = me - 2 * sign * step

        @pl.when(within(z - sign * step))
        def _():
            pl.when(step > 0)(lambda: copy(source, way, beside).wait_recv())
            pl.when(within(z + sign))(lambda: copy(source, way, me + 2 * sign).start())
            pl.when(i != 1)(lambda: copy(source, 2, beside).start())

        @pl.when(way == 1)
        def _():
            for j in range(2):
                query_copy(j, step).start()

    @pl.loop(0, line)
    def _(level):
        copy(level * 2 + 1 - x, 2, beside).wait_recv()
        for j in range(2):
            query_copy(j, level).wait()

    @pl.loop(0, 2 * line)
    def _(i):
        step, way = lax.div(i, 2), lax.rem(i, 2)
        sign = 1 - 2 * way
        source = me - 2 * sign * step

        @pl.when(within(z - sign * step))
        def _():
            pl.when(within(z + sign))(lambda: copy(source, way, beside).wait_send())
            pl.when(i != 1)(lambda: copy(source, 2, beside).wait_send())


def move(shards, masks, queries, own_kv):
    rows, width = queries.shape
    return pl.pallas_call(
        functools.partial(move_kernel, shards, masks),
        out_shape=(
            jax.ShapeDtypeStruct((rows, width), jnp.bfloat16),
            jax.ShapeDtypeStruct((shards,) + own_kv.shape, jnp.bfloat16),
        ),
        in_specs=[pl.BlockSpec(memory_space=pl.ANY)] * 2,
        out_specs=(pl.BlockSpec(memory_space=pl.ANY),) * 2,
        scratch_shapes=[
            pltpu.SemaphoreType.DMA,
            pltpu.SemaphoreType.DMA((2, shards // 2)),
            pltpu.SemaphoreType.DMA((2, shards // 2)),
            pltpu.SemaphoreType.DMA((shards, 3)),
            pltpu.SemaphoreType.DMA((shards,)),
        ],
        compiler_params=pltpu.CompilerParams(
            collective_id=(masks[0] - 1) * (shards - 1) + masks[1] - 1, has_side_effects=True
        ),
        name=f"move_{masks[0]}_{masks[1]}",
    )(queries, own_kv)


def attend_kernel(placement, lengths, steer_index, q_ref, kv_ref, steering_ref, out_ref, acc, top):
    me = lax.axis_index("ctx")
    rows = q_ref.shape[0]
    heads = q_ref.shape[1] // HD
    requests = lengths.shape[0]
    half = rows // 2
    first = me * rows
    ends = []
    for r in range(requests):
        ends.append(lengths[r] + (ends[-1] if r else 0))

    row_pos = first + lax.broadcasted_iota(jnp.int32, (rows, 1), 0)
    row_start = jnp.zeros((rows, 1), jnp.int32)
    first_start = jnp.int32(0)
    for r in range(requests):
        row_start = row_start + jnp.where(row_pos >= ends[r], lengths[r], 0)
        first_start = first_start + jnp.where(first >= ends[r], lengths[r], 0)

    top[...] = jnp.full(top.shape, FILL, jnp.float32)
    acc[...] = jnp.zeros(acc.shape, jnp.float32)

    def block(index, carry):
        at = index * rows
        upper = kv_ref.at[jnp.bitwise_xor(index, placement[0])]
        lower = kv_ref.at[jnp.bitwise_xor(index, placement[1])]
        key = jnp.concatenate([upper[0, :half], lower[0, half:]], axis=0)
        value = jnp.concatenate([upper[1, :half], lower[1, half:]], axis=0)
        value = jnp.concatenate([value, jnp.ones_like(value)], axis=1)
        key_pos = at + lax.broadcasted_iota(jnp.int32, (rows, rows), 1)
        bias = jnp.where((key_pos >= row_start) & (key_pos <= row_pos), 0.0, FILL)
        for h in range(heads):
            query = q_ref[:, h * HD : (h + 1) * HD]
            scores = bias + lax.dot_general(
                query, key, (((1,), (1,)), ((), ())), preferred_element_type=jnp.float32
            )
            old = top[h]
            new = jnp.maximum(old, jnp.max(scores, axis=1, keepdims=True))
            rescale = jnp.exp2((old - new) * FACTOR)
            top[h] = new
            weights = jnp.exp2((scores - jnp.concatenate([new] * (rows // HD), axis=1)) * FACTOR)
            acc[h] = acc[h] * jnp.concatenate([rescale, rescale], axis=1) + jnp.dot(
                weights.astype(jnp.bfloat16), value, preferred_element_type=jnp.float32
            )
        return carry

    lax.fori_loop(lax.div(first_start, rows), me + 1, block, 0)

    vectors = steering_ref.shape[0]
    pos = first + lax.broadcasted_iota(jnp.int32, (rows, vectors), 0)
    chosen = jnp.zeros((rows, vectors), jnp.int32)
    for r in range(requests):
        inside = (pos >= ends[r] - lengths[r]) & (pos < ends[r])
        chosen = jnp.where(inside, steer_index[r], chosen)
    one_hot = (chosen == lax.broadcasted_iota(jnp.int32, (rows, vectors), 1)).astype(jnp.bfloat16)
    for h in range(heads):
        columns = slice(h * HD, (h + 1) * HD)
        mixed = (acc[h, :, :HD] / acc[h, :, HD:]).astype(jnp.bfloat16)
        steer = jnp.dot(one_hot, steering_ref[:, columns], preferred_element_type=jnp.float32)
        out_ref[:, columns] = (mixed.astype(jnp.float32) + steer).astype(jnp.bfloat16)


def attend(queries, kv, placement, lengths, steer_index, steering):
    rows, width = queries.shape
    heads = width // HD
    vmem = pl.BlockSpec(memory_space=pltpu.VMEM)
    smem = pl.BlockSpec(memory_space=pltpu.SMEM)
    return pl.pallas_call(
        attend_kernel,
        out_shape=jax.ShapeDtypeStruct((rows, width), jnp.bfloat16),
        in_specs=[smem, smem, smem, vmem, vmem, vmem],
        out_specs=vmem,
        scratch_shapes=[
            pltpu.VMEM((heads, rows, 2 * HD), jnp.float32),
            pltpu.VMEM((heads, rows, HD), jnp.float32),
        ],
        compiler_params=pltpu.CompilerParams(vmem_limit_bytes=48 * 2**20),
        name="attend",
    )(placement, lengths, steer_index, queries, kv, steering)


def move_by_bits(shards, queries, own_kv, placement):
    rows = queries.shape[0]
    first_half = jnp.arange(rows) < rows // 2
    bit = 1
    while bit < shards:
        pairs = [(source, source ^ bit) for source in range(shards)]
        moved = lax.ppermute(queries, "ctx", pairs)
        flags = (placement // bit) % 2
        queries = jnp.where(
            (jnp.where(first_half, flags[0], flags[1]) == 1)[:, None], moved, queries
        )
        bit *= 2
    return queries, lax.all_gather(own_kv, "ctx")


def choose(branches, low, chosen, *operands):
    if len(branches) == 1:
        return branches[0](*operands)
    middle = len(branches) // 2
    return lax.cond(
        chosen < low + middle,
        functools.partial(choose, branches[:middle], low),
        functools.partial(choose, branches[middle:], low + middle),
        chosen,
        *operands,
    )


def body(queries, keys_values, placement, lengths, steer_index, steering):
    shards = lax.axis_size("ctx")
    own_kv = keys_values.transpose(1, 0, 2)
    if shards <= 8:
        count = shards - 1
        branches = [
            functools.partial(move, shards, (1 + i // count, 1 + i % count))
            for i in range(count * count)
        ]
        chosen = jnp.sum((placement - 1) * jnp.array([count, 1], jnp.int32))
        queries, kv = choose(branches, 0, chosen, queries, own_kv)
    else:
        queries, kv = move_by_bits(shards, queries, own_kv, placement)
    return attend(queries, kv, placement, lengths, steer_index, steering)


def solution(mesh):
    return jax.shard_map(
        body,
        mesh=mesh,
        in_specs=(P("ctx", "tp"), P("ctx", None, "tp"), P(), P(), P(), P(None, "tp")),
        out_specs=P("ctx", "tp"),
        check_vma=False,
    )
```

```python
import functools
import math

import jax
import jax.numpy as jnp
from jax import lax
from jax.experimental import pallas as pl
from jax.experimental.pallas import tpu as pltpu
from jax.sharding import PartitionSpec as P

HD = 128
FILL = -1e30
FACTOR = math.log2(math.e) / math.sqrt(HD)
MESH = pl.DeviceIdType.MESH


def flip(value, mask):
    result = value
    bit = 1
    while bit <= mask:
        if mask & bit:
            result = result + bit * (1 - 2 * lax.rem(lax.div(value, bit), 2))
        bit *= 2
    return result


def move_kernel(shards, masks, q_ref, kv_ref, q_out, kv_out, own_sem, q_send, q_recv, kv_send, kv_recv):
    me = lax.axis_index("ctx")
    own_copy = pltpu.make_async_copy(kv_ref, kv_out.at[me], own_sem)
    own_copy.start()
    barrier = pltpu.get_barrier_semaphore()

    @pl.loop(1, shards)
    def _(away):
        pl.semaphore_signal(
            barrier, inc=1, device_id={"ctx": lax.rem(me + away, shards)}, device_id_type=MESH
        )

    pl.semaphore_wait(barrier, shards - 1)
    own_copy.wait()

    half = q_ref.shape[0] // 2
    line = shards // 2
    part = half // line
    x, z = lax.rem(me, 2), lax.div(me, 2)
    beside = me + 1 - 2 * x

    def copy(source, way, target):
        return pltpu.make_async_remote_copy(
            src_ref=kv_out.at[source],
            dst_ref=kv_out.at[source],
            send_sem=kv_send.at[source, way],
            recv_sem=kv_recv.at[source],
            device_id={"ctx": target},
            device_id_type=MESH,
        )

    def query_copy(j, c):
        rows = pl.ds(pl.multiple_of(j * half + c * part, part), part)
        return pltpu.make_async_remote_copy(
            src_ref=q_ref.at[rows],
            dst_ref=q_out.at[rows],
            send_sem=q_send.at[j, c],
            recv_sem=q_recv.at[j, c],
            device_id={"ctx": flip(me, masks[j])},
            device_id_type=MESH,
        )

    def within(level):
        return lax.div(level + line, line) == 1

    @pl.loop(0, 2 * line)
    def _(i):
        step, way = lax.div(i, 2), lax.rem(i, 2)
        sign = 1 - 2 * way
        source = me - 2 * sign * step

        @pl.when(within(z - sign * step))
        def _():
            pl.when(step > 0)(lambda: copy(source, way, beside).wait_recv())
            pl.when(within(z + sign))(lambda: copy(source, way, me + 2 * sign).start())
            pl.when(i != 1)(lambda: copy(source, 2, beside).start())

        @pl.when(way * step >= 1)
        def _():
            for j in range(2):
                query_copy(j, step - 1).start()

        @pl.when(i == 2 * line - 3)
        def _():
            for j in range(2):
                query_copy(j, line - 1).start()

    @pl.loop(0, line)
    def _(level):
        copy(level * 2 + 1 - x, 2, beside).wait_recv()
        for j in range(2):
            query_copy(j, level).wait()

    @pl.loop(0, 2 * line)
    def _(i):
        step, way = lax.div(i, 2), lax.rem(i, 2)
        sign = 1 - 2 * way
        source = me - 2 * sign * step

        @pl.when(within(z - sign * step))
        def _():
            pl.when(within(z + sign))(lambda: copy(source, way, beside).wait_send())
            pl.when(i != 1)(lambda: copy(source, 2, beside).wait_send())


def move(shards, masks, queries, own_kv):
    rows, width = queries.shape
    return pl.pallas_call(
        functools.partial(move_kernel, shards, masks),
        out_shape=(
            jax.ShapeDtypeStruct((rows, width), jnp.bfloat16),
            jax.ShapeDtypeStruct((shards,) + own_kv.shape, jnp.bfloat16),
        ),
        in_specs=[pl.BlockSpec(memory_space=pl.ANY)] * 2,
        out_specs=(pl.BlockSpec(memory_space=pl.ANY),) * 2,
        scratch_shapes=[
            pltpu.SemaphoreType.DMA,
            pltpu.SemaphoreType.DMA((2, shards // 2)),
            pltpu.SemaphoreType.DMA((2, shards // 2)),
            pltpu.SemaphoreType.DMA((shards, 3)),
            pltpu.SemaphoreType.DMA((shards,)),
        ],
        compiler_params=pltpu.CompilerParams(
            collective_id=(masks[0] - 1) * (shards - 1) + masks[1] - 1, has_side_effects=True
        ),
        name=f"move_{masks[0]}_{masks[1]}",
    )(queries, own_kv)


def attend_kernel(placement, lengths, steer_index, q_ref, kv_ref, steering_ref, out_ref, acc, top):
    me = lax.axis_index("ctx")
    rows = q_ref.shape[0]
    heads = q_ref.shape[1] // HD
    requests = lengths.shape[0]
    half = rows // 2
    first = me * rows
    ends = []
    for r in range(requests):
        ends.append(lengths[r] + (ends[-1] if r else 0))

    row_pos = first + lax.broadcasted_iota(jnp.int32, (rows, 1), 0)
    row_start = jnp.zeros((rows, 1), jnp.int32)
    first_start = jnp.int32(0)
    for r in range(requests):
        row_start = row_start + jnp.where(row_pos >= ends[r], lengths[r], 0)
        first_start = first_start + jnp.where(first >= ends[r], lengths[r], 0)

    @pl.loop(0, heads)
    def _(h):
        top[h] = jnp.full(top.shape[1:], FILL, jnp.float32)
        acc[h] = jnp.zeros(acc.shape[1:], jnp.float32)

    group = math.gcd(heads, 4)

    def head(h, key, value, bias):
        query = q_ref[:, pl.ds(pl.multiple_of(h * HD, HD), HD)]
        scores = bias + lax.dot_general(
            query, key, (((1,), (1,)), ((), ())), preferred_element_type=jnp.float32
        )
        old = top[h]
        new = jnp.maximum(old, jnp.max(scores, axis=1, keepdims=True))
        rescale = jnp.exp2((old - new) * FACTOR)
        top[h] = new
        weights = jnp.exp2((scores - jnp.concatenate([new] * (rows // HD), axis=1)) * FACTOR)
        acc[h] = acc[h] * jnp.concatenate([rescale, rescale], axis=1) + jnp.dot(
            weights.astype(jnp.bfloat16), value, preferred_element_type=jnp.float32
        )

    def block(index, carry):
        at = index * rows
        upper = kv_ref.at[jnp.bitwise_xor(index, placement[0])]
        lower = kv_ref.at[jnp.bitwise_xor(index, placement[1])]
        key = jnp.concatenate([upper[0, :half], lower[0, half:]], axis=0)
        value = jnp.concatenate([upper[1, :half], lower[1, half:]], axis=0)
        value = jnp.concatenate([value, jnp.ones_like(value)], axis=1)
        key_pos = at + lax.broadcasted_iota(jnp.int32, (rows, rows), 1)
        bias = jnp.where((key_pos >= row_start) & (key_pos <= row_pos), 0.0, FILL)
        @pl.loop(0, heads // group)
        def _(turn):
            for member in range(group):
                head(turn * group + member, key, value, bias)

        return carry

    lax.fori_loop(lax.div(first_start, rows), me + 1, block, 0)

    vectors = steering_ref.shape[0]
    pos = first + lax.broadcasted_iota(jnp.int32, (rows, vectors), 0)
    chosen = jnp.zeros((rows, vectors), jnp.int32)
    for r in range(requests):
        inside = (pos >= ends[r] - lengths[r]) & (pos < ends[r])
        chosen = jnp.where(inside, steer_index[r], chosen)
    one_hot = (chosen == lax.broadcasted_iota(jnp.int32, (rows, vectors), 1)).astype(jnp.bfloat16)

    @pl.loop(0, heads)
    def _(h):
        columns = pl.ds(pl.multiple_of(h * HD, HD), HD)
        mixed = (acc[h, :, :HD] / acc[h, :, HD:]).astype(jnp.bfloat16)
        steer = jnp.dot(one_hot, steering_ref[:, columns], preferred_element_type=jnp.float32)
        out_ref[:, columns] = (mixed.astype(jnp.float32) + steer).astype(jnp.bfloat16)


def attend(queries, kv, placement, lengths, steer_index, steering):
    rows, width = queries.shape
    heads = width // HD
    vmem = pl.BlockSpec(memory_space=pltpu.VMEM)
    smem = pl.BlockSpec(memory_space=pltpu.SMEM)
    return pl.pallas_call(
        attend_kernel,
        out_shape=jax.ShapeDtypeStruct((rows, width), jnp.bfloat16),
        in_specs=[smem, smem, smem, vmem, vmem, vmem],
        out_specs=vmem,
        scratch_shapes=[
            pltpu.VMEM((heads, rows, 2 * HD), jnp.float32),
            pltpu.VMEM((heads, rows, HD), jnp.float32),
        ],
        compiler_params=pltpu.CompilerParams(vmem_limit_bytes=48 * 2**20),
        name="attend",
    )(placement, lengths, steer_index, queries, kv, steering)


def move_by_bits(shards, queries, own_kv, placement):
    rows = queries.shape[0]
    first_half = jnp.arange(rows) < rows // 2
    bit = 1
    while bit < shards:
        pairs = [(source, source ^ bit) for source in range(shards)]
        moved = lax.ppermute(queries, "ctx", pairs)
        flags = (placement // bit) % 2
        queries = jnp.where(
            (jnp.where(first_half, flags[0], flags[1]) == 1)[:, None], moved, queries
        )
        bit *= 2
    return queries, lax.all_gather(own_kv, "ctx")


def body(queries, keys_values, placement, lengths, steer_index, steering):
    shards = lax.axis_size("ctx")
    own_kv = keys_values.transpose(1, 0, 2)
    if shards <= 8:
        count = shards - 1
        branches = [
            functools.partial(move, shards, (1 + i // count, 1 + i % count))
            for i in range(count * count)
        ]
        chosen = jnp.sum((placement - 1) * jnp.array([count, 1], jnp.int32))
        queries, kv = lax.switch(chosen, branches, queries, own_kv)
    else:
        queries, kv = move_by_bits(shards, queries, own_kv, placement)
    return attend(queries, kv, placement, lengths, steer_index, steering)


def solution(mesh):
    return jax.shard_map(
        body,
        mesh=mesh,
        in_specs=(P("ctx", "tp"), P("ctx", None, "tp"), P(), P(), P(), P(None, "tp")),
        out_specs=P("ctx", "tp"),
        check_vma=False,
    )
```

```python
import functools
import math

import jax
import jax.numpy as jnp
from jax import lax
from jax.experimental import pallas as pl
from jax.experimental.pallas import tpu as pltpu
from jax.sharding import PartitionSpec as P

HD = 128
FILL = -1e30
FACTOR = math.log2(math.e) / math.sqrt(HD)
MESH = pl.DeviceIdType.MESH


def flip(value, mask):
    result = value
    bit = 1
    while bit <= mask:
        if mask & bit:
            result = result + bit * (1 - 2 * lax.rem(lax.div(value, bit), 2))
        bit *= 2
    return result


def move_kernel(shards, masks, q_ref, kv_ref, q_out, kv_out, own_sem, q_send, q_recv, kv_send, kv_recv):
    me = lax.axis_index("ctx")
    own_copy = pltpu.make_async_copy(kv_ref, kv_out.at[me], own_sem)
    own_copy.start()
    barrier = pltpu.get_barrier_semaphore()

    @pl.loop(1, shards)
    def _(away):
        pl.semaphore_signal(
            barrier, inc=1, device_id={"ctx": lax.rem(me + away, shards)}, device_id_type=MESH
        )

    pl.semaphore_wait(barrier, shards - 1)
    own_copy.wait()

    half = q_ref.shape[0] // 2
    line = shards // 2
    part = half // line
    x, z = lax.rem(me, 2), lax.div(me, 2)
    beside = me + 1 - 2 * x

    def copy(source, way, target):
        return pltpu.make_async_remote_copy(
            src_ref=kv_out.at[source],
            dst_ref=kv_out.at[source],
            send_sem=kv_send.at[source, way],
            recv_sem=kv_recv.at[source],
            device_id={"ctx": target},
            device_id_type=MESH,
        )

    def query_copy(j, c):
        rows = pl.ds(pl.multiple_of(j * half + c * part, part), part)
        return pltpu.make_async_remote_copy(
            src_ref=q_ref.at[rows],
            dst_ref=q_out.at[rows],
            send_sem=q_send.at[j, c],
            recv_sem=q_recv.at[j, c],
            device_id={"ctx": flip(me, masks[j])},
            device_id_type=MESH,
        )

    def within(level):
        return lax.div(level + line, line) == 1

    @pl.loop(0, 2 * line)
    def _(i):
        step, way = lax.div(i, 2), lax.rem(i, 2)
        sign = 1 - 2 * way
        source = me - 2 * sign * step

        @pl.when(within(z - sign * step))
        def _():
            pl.when(step > 0)(lambda: copy(source, way, beside).wait_recv())
            pl.when(within(z + sign))(lambda: copy(source, way, me + 2 * sign).start())
            pl.when(i != 1)(lambda: copy(source, 2, beside).start())

        @pl.when(way * step >= 1)
        def _():
            for j in range(2):
                query_copy(j, step - 1).start()

        @pl.when(i == 2 * line - 3)
        def _():
            for j in range(2):
                query_copy(j, line - 1).start()

    @pl.loop(0, line)
    def _(level):
        copy(level * 2 + 1 - x, 2, beside).wait_recv()
        for j in range(2):
            query_copy(j, level).wait()

    @pl.loop(0, 2 * line)
    def _(i):
        step, way = lax.div(i, 2), lax.rem(i, 2)
        sign = 1 - 2 * way
        source = me - 2 * sign * step

        @pl.when(within(z - sign * step))
        def _():
            pl.when(within(z + sign))(lambda: copy(source, way, beside).wait_send())
            pl.when(i != 1)(lambda: copy(source, 2, beside).wait_send())


def move(shards, masks, queries, own_kv):
    rows, width = queries.shape
    return pl.pallas_call(
        functools.partial(move_kernel, shards, masks),
        out_shape=(
            jax.ShapeDtypeStruct((rows, width), jnp.bfloat16),
            jax.ShapeDtypeStruct((shards,) + own_kv.shape, jnp.bfloat16),
        ),
        in_specs=[pl.BlockSpec(memory_space=pl.ANY)] * 2,
        out_specs=(pl.BlockSpec(memory_space=pl.ANY),) * 2,
        scratch_shapes=[
            pltpu.SemaphoreType.DMA,
            pltpu.SemaphoreType.DMA((2, shards // 2)),
            pltpu.SemaphoreType.DMA((2, shards // 2)),
            pltpu.SemaphoreType.DMA((shards, 3)),
            pltpu.SemaphoreType.DMA((shards,)),
        ],
        compiler_params=pltpu.CompilerParams(
            collective_id=(masks[0] - 1) * (shards - 1) + masks[1] - 1, has_side_effects=True
        ),
        name=f"move_{masks[0]}_{masks[1]}",
    )(queries, own_kv)


def attend_kernel(placement, lengths, steer_index, q_ref, kv_ref, steering_ref, out_ref, acc, top):
    me = lax.axis_index("ctx")
    rows = q_ref.shape[0]
    heads = q_ref.shape[1] // HD
    requests = lengths.shape[0]
    half = rows // 2
    first = me * rows
    ends = []
    for r in range(requests):
        ends.append(lengths[r] + (ends[-1] if r else 0))

    row_pos = first + lax.broadcasted_iota(jnp.int32, (rows, 1), 0)
    row_start = jnp.zeros((rows, 1), jnp.int32)
    first_start = jnp.int32(0)
    for r in range(requests):
        row_start = row_start + jnp.where(row_pos >= ends[r], lengths[r], 0)
        first_start = first_start + jnp.where(first >= ends[r], lengths[r], 0)

    @pl.loop(0, heads)
    def _(h):
        top[h] = jnp.full(top.shape[1:], FILL, jnp.float32)
        acc[h] = jnp.zeros(acc.shape[1:], jnp.float32)

    def head(h, key, value, bias):
        query = q_ref[:, h * HD : (h + 1) * HD]
        scores = bias + lax.dot_general(
            query, key, (((1,), (1,)), ((), ())), preferred_element_type=jnp.float32
        )
        old = top[h]
        new = jnp.maximum(old, jnp.max(scores, axis=1, keepdims=True))
        rescale = jnp.exp2((old - new) * FACTOR)
        top[h] = new
        weights = jnp.exp2((scores - jnp.concatenate([new] * (rows // HD), axis=1)) * FACTOR)
        acc[h] = acc[h] * jnp.concatenate([rescale, rescale], axis=1) + jnp.dot(
            weights.astype(jnp.bfloat16), value, preferred_element_type=jnp.float32
        )

    def block(index, carry):
        at = index * rows
        upper = kv_ref.at[jnp.bitwise_xor(index, placement[0])]
        lower = kv_ref.at[jnp.bitwise_xor(index, placement[1])]
        key = jnp.concatenate([upper[0, :half], lower[0, half:]], axis=0)
        value = jnp.concatenate([upper[1, :half], lower[1, half:]], axis=0)
        value = jnp.concatenate([value, jnp.ones_like(value)], axis=1)
        key_pos = at + lax.broadcasted_iota(jnp.int32, (rows, rows), 1)
        bias = jnp.where((key_pos >= row_start) & (key_pos <= row_pos), 0.0, FILL)
        for h in range(heads):
            head(h, key, value, bias)

        return carry

    lax.fori_loop(lax.div(first_start, rows), me + 1, block, 0)

    vectors = steering_ref.shape[0]
    pos = first + lax.broadcasted_iota(jnp.int32, (rows, vectors), 0)
    chosen = jnp.zeros((rows, vectors), jnp.int32)
    for r in range(requests):
        inside = (pos >= ends[r] - lengths[r]) & (pos < ends[r])
        chosen = jnp.where(inside, steer_index[r], chosen)
    one_hot = (chosen == lax.broadcasted_iota(jnp.int32, (rows, vectors), 1)).astype(jnp.bfloat16)
    for h in range(heads):
        columns = slice(h * HD, (h + 1) * HD)
        mixed = (acc[h, :, :HD] / acc[h, :, HD:]).astype(jnp.bfloat16)
        steer = jnp.dot(one_hot, steering_ref[:, columns], preferred_element_type=jnp.float32)
        out_ref[:, columns] = (mixed.astype(jnp.float32) + steer).astype(jnp.bfloat16)


def attend(queries, kv, placement, lengths, steer_index, steering):
    rows, width = queries.shape
    heads = width // HD
    vmem = pl.BlockSpec(memory_space=pltpu.VMEM)
    smem = pl.BlockSpec(memory_space=pltpu.SMEM)
    return pl.pallas_call(
        attend_kernel,
        out_shape=jax.ShapeDtypeStruct((rows, width), jnp.bfloat16),
        in_specs=[smem, smem, smem, vmem, vmem, vmem],
        out_specs=vmem,
        scratch_shapes=[
            pltpu.VMEM((heads, rows, 2 * HD), jnp.float32),
            pltpu.VMEM((heads, rows, HD), jnp.float32),
        ],
        compiler_params=pltpu.CompilerParams(vmem_limit_bytes=48 * 2**20),
        name="attend",
    )(placement, lengths, steer_index, queries, kv, steering)


def move_by_bits(shards, queries, own_kv, placement):
    rows = queries.shape[0]
    first_half = jnp.arange(rows) < rows // 2
    bit = 1
    while bit < shards:
        pairs = [(source, source ^ bit) for source in range(shards)]
        moved = lax.ppermute(queries, "ctx", pairs)
        flags = (placement // bit) % 2
        queries = jnp.where(
            (jnp.where(first_half, flags[0], flags[1]) == 1)[:, None], moved, queries
        )
        bit *= 2
    return queries, lax.all_gather(own_kv, "ctx")


def body(queries, keys_values, placement, lengths, steer_index, steering):
    shards = lax.axis_size("ctx")
    own_kv = keys_values.transpose(1, 0, 2)
    if shards <= 8:
        count = shards - 1
        branches = [
            functools.partial(move, shards, (1 + i // count, 1 + i % count))
            for i in range(count * count)
        ]
        chosen = jnp.sum((placement - 1) * jnp.array([count, 1], jnp.int32))
        queries, kv = lax.switch(chosen, branches, queries, own_kv)
    else:
        queries, kv = move_by_bits(shards, queries, own_kv, placement)
    return attend(queries, kv, placement, lengths, steer_index, steering)


def solution(mesh):
    return jax.shard_map(
        body,
        mesh=mesh,
        in_specs=(P("ctx", "tp"), P("ctx", None, "tp"), P(), P(), P(), P(None, "tp")),
        out_specs=P("ctx", "tp"),
        check_vma=False,
    )
```

```python
import functools
import math

import jax
import jax.numpy as jnp
from jax import lax
from jax.experimental import pallas as pl
from jax.experimental.pallas import tpu as pltpu
from jax.sharding import PartitionSpec as P

HD = 128
FILL = -1e30
FACTOR = math.log2(math.e) / math.sqrt(HD)
MESH = pl.DeviceIdType.MESH


def flip(value, mask):
    result = value
    bit = 1
    while bit <= mask:
        if mask & bit:
            result = result + bit * (1 - 2 * lax.rem(lax.div(value, bit), 2))
        bit *= 2
    return result


def move_kernel(shards, masks, q_ref, kv_ref, q_out, kv_out, own_sem, q_send, q_recv, kv_send, kv_recv):
    me = lax.axis_index("ctx")
    own_copy = pltpu.make_async_copy(kv_ref, kv_out.at[me], own_sem)
    own_copy.start()
    barrier = pltpu.get_barrier_semaphore()

    @pl.loop(1, shards)
    def _(away):
        pl.semaphore_signal(
            barrier, inc=1, device_id={"ctx": lax.rem(me + away, shards)}, device_id_type=MESH
        )

    pl.semaphore_wait(barrier, shards - 1)
    own_copy.wait()

    half = q_ref.shape[0] // 2
    line = shards // 2
    part = half // line
    x, z = lax.rem(me, 2), lax.div(me, 2)
    beside = me + 1 - 2 * x

    def copy(source, way, target):
        return pltpu.make_async_remote_copy(
            src_ref=kv_out.at[source],
            dst_ref=kv_out.at[source],
            send_sem=kv_send.at[source, way],
            recv_sem=kv_recv.at[source],
            device_id={"ctx": target},
            device_id_type=MESH,
        )

    def query_copy(j, c):
        rows = pl.ds(pl.multiple_of(j * half + c * part, part), part)
        return pltpu.make_async_remote_copy(
            src_ref=q_ref.at[rows],
            dst_ref=q_out.at[rows],
            send_sem=q_send.at[j, c],
            recv_sem=q_recv.at[j, c],
            device_id={"ctx": flip(me, masks[j])},
            device_id_type=MESH,
        )

    def within(level):
        return lax.div(level + line, line) == 1

    @pl.loop(0, 2 * line)
    def _(i):
        step, way = lax.div(i, 2), lax.rem(i, 2)
        sign = 1 - 2 * way
        source = me - 2 * sign * step

        @pl.when(within(z - sign * step))
        def _():
            pl.when(step > 0)(lambda: copy(source, way, beside).wait_recv())
            pl.when(within(z + sign))(lambda: copy(source, way, me + 2 * sign).start())
            pl.when(i != 1)(lambda: copy(source, 2, beside).start())

        @pl.when(lax.div(way * step + 1, 2) == 1)
        def _():
            for j in range(2):
                for c in range(2):
                    query_copy(j, 2 * step - 2 + c).start()

    @pl.loop(0, line)
    def _(level):
        copy(level * 2 + 1 - x, 2, beside).wait_recv()
        for j in range(2):
            query_copy(j, level).wait()

    @pl.loop(0, 2 * line)
    def _(i):
        step, way = lax.div(i, 2), lax.rem(i, 2)
        sign = 1 - 2 * way
        source = me - 2 * sign * step

        @pl.when(within(z - sign * step))
        def _():
            pl.when(within(z + sign))(lambda: copy(source, way, beside).wait_send())
            pl.when(i != 1)(lambda: copy(source, 2, beside).wait_send())


def move(shards, masks, queries, own_kv):
    rows, width = queries.shape
    return pl.pallas_call(
        functools.partial(move_kernel, shards, masks),
        out_shape=(
            jax.ShapeDtypeStruct((rows, width), jnp.bfloat16),
            jax.ShapeDtypeStruct((shards,) + own_kv.shape, jnp.bfloat16),
        ),
        in_specs=[pl.BlockSpec(memory_space=pl.ANY)] * 2,
        out_specs=(pl.BlockSpec(memory_space=pl.ANY),) * 2,
        scratch_shapes=[
            pltpu.SemaphoreType.DMA,
            pltpu.SemaphoreType.DMA((2, shards // 2)),
            pltpu.SemaphoreType.DMA((2, shards // 2)),
            pltpu.SemaphoreType.DMA((shards, 3)),
            pltpu.SemaphoreType.DMA((shards,)),
        ],
        compiler_params=pltpu.CompilerParams(
            collective_id=(masks[0] - 1) * (shards - 1) + masks[1] - 1, has_side_effects=True
        ),
        name=f"move_{masks[0]}_{masks[1]}",
    )(queries, own_kv)


def attend_kernel(placement, lengths, steer_index, q_ref, kv_ref, steering_ref, out_ref, acc, top):
    me = lax.axis_index("ctx")
    rows = q_ref.shape[0]
    heads = q_ref.shape[1] // HD
    requests = lengths.shape[0]
    half = rows // 2
    first = me * rows
    ends = []
    for r in range(requests):
        ends.append(lengths[r] + (ends[-1] if r else 0))

    row_pos = first + lax.broadcasted_iota(jnp.int32, (rows, 1), 0)
    row_start = jnp.zeros((rows, 1), jnp.int32)
    first_start = jnp.int32(0)
    for r in range(requests):
        row_start = row_start + jnp.where(row_pos >= ends[r], lengths[r], 0)
        first_start = first_start + jnp.where(first >= ends[r], lengths[r], 0)

    @pl.loop(0, heads)
    def _(h):
        top[h] = jnp.full(top.shape[1:], FILL, jnp.float32)
        acc[h] = jnp.zeros(acc.shape[1:], jnp.float32)

    def head(h, key, value, bias):
        query = q_ref[:, h * HD : (h + 1) * HD]
        scores = bias + lax.dot_general(
            query, key, (((1,), (1,)), ((), ())), preferred_element_type=jnp.float32
        )
        old = top[h]
        new = jnp.maximum(old, jnp.max(scores, axis=1, keepdims=True))
        rescale = jnp.exp2((old - new) * FACTOR)
        top[h] = new
        weights = jnp.exp2((scores - jnp.concatenate([new] * (rows // HD), axis=1)) * FACTOR)
        acc[h] = acc[h] * jnp.concatenate([rescale, rescale], axis=1) + jnp.dot(
            weights.astype(jnp.bfloat16), value, preferred_element_type=jnp.float32
        )

    def block(index, carry):
        at = index * rows
        upper = kv_ref.at[jnp.bitwise_xor(index, placement[0])]
        lower = kv_ref.at[jnp.bitwise_xor(index, placement[1])]
        key = jnp.concatenate([upper[0, :half], lower[0, half:]], axis=0)
        value = jnp.concatenate([upper[1, :half], lower[1, half:]], axis=0)
        value = jnp.concatenate([value, jnp.ones_like(value)], axis=1)
        key_pos = at + lax.broadcasted_iota(jnp.int32, (rows, rows), 1)
        bias = jnp.where((key_pos >= row_start) & (key_pos <= row_pos), 0.0, FILL)
        for h in range(heads):
            head(h, key, value, bias)

        return carry

    lax.fori_loop(lax.div(first_start, rows), me + 1, block, 0)

    vectors = steering_ref.shape[0]
    pos = first + lax.broadcasted_iota(jnp.int32, (rows, vectors), 0)
    chosen = jnp.zeros((rows, vectors), jnp.int32)
    for r in range(requests):
        inside = (pos >= ends[r] - lengths[r]) & (pos < ends[r])
        chosen = jnp.where(inside, steer_index[r], chosen)
    one_hot = (chosen == lax.broadcasted_iota(jnp.int32, (rows, vectors), 1)).astype(jnp.bfloat16)
    for h in range(heads):
        columns = slice(h * HD, (h + 1) * HD)
        mixed = (acc[h, :, :HD] / acc[h, :, HD:]).astype(jnp.bfloat16)
        steer = jnp.dot(one_hot, steering_ref[:, columns], preferred_element_type=jnp.float32)
        out_ref[:, columns] = (mixed.astype(jnp.float32) + steer).astype(jnp.bfloat16)


def attend(queries, kv, placement, lengths, steer_index, steering):
    rows, width = queries.shape
    heads = width // HD
    vmem = pl.BlockSpec(memory_space=pltpu.VMEM)
    smem = pl.BlockSpec(memory_space=pltpu.SMEM)
    return pl.pallas_call(
        attend_kernel,
        out_shape=jax.ShapeDtypeStruct((rows, width), jnp.bfloat16),
        in_specs=[smem, smem, smem, vmem, vmem, vmem],
        out_specs=vmem,
        scratch_shapes=[
            pltpu.VMEM((heads, rows, 2 * HD), jnp.float32),
            pltpu.VMEM((heads, rows, HD), jnp.float32),
        ],
        compiler_params=pltpu.CompilerParams(vmem_limit_bytes=48 * 2**20),
        name="attend",
    )(placement, lengths, steer_index, queries, kv, steering)


def move_by_bits(shards, queries, own_kv, placement):
    rows = queries.shape[0]
    first_half = jnp.arange(rows) < rows // 2
    bit = 1
    while bit < shards:
        pairs = [(source, source ^ bit) for source in range(shards)]
        moved = lax.ppermute(queries, "ctx", pairs)
        flags = (placement // bit) % 2
        queries = jnp.where(
            (jnp.where(first_half, flags[0], flags[1]) == 1)[:, None], moved, queries
        )
        bit *= 2
    return queries, lax.all_gather(own_kv, "ctx")


def body(queries, keys_values, placement, lengths, steer_index, steering):
    shards = lax.axis_size("ctx")
    own_kv = keys_values.transpose(1, 0, 2)
    if shards <= 8:
        count = shards - 1
        branches = [
            functools.partial(move, shards, (1 + i // count, 1 + i % count))
            for i in range(count * count)
        ]
        chosen = jnp.sum((placement - 1) * jnp.array([count, 1], jnp.int32))
        queries, kv = lax.switch(chosen, branches, queries, own_kv)
    else:
        queries, kv = move_by_bits(shards, queries, own_kv, placement)
    return attend(queries, kv, placement, lengths, steer_index, steering)


def solution(mesh):
    return jax.shard_map(
        body,
        mesh=mesh,
        in_specs=(P("ctx", "tp"), P("ctx", None, "tp"), P(), P(), P(), P(None, "tp")),
        out_specs=P("ctx", "tp"),
        check_vma=False,
    )
```
